32 devices in a mesh: leaf: 8 (over z, y), rep: 4 (over x, core).
Axes of the slice: x: 2, y: 2, z: 4, core: 2. Of those that a mesh axis runs over, the one named last changes fastest.
Arguments:
- panel_feats: bfloat16 [24576, 2, 1024], P('leaf', None, 'rep'), may hold values from -6 to 6
- panel_dest: int32 [24576], P('leaf'), may hold values from 0 to 24575, as said below
- coefs: float32 [1024], P('rep'), may hold values from -2 to 2
- sketch_left: bfloat16 [512, 64], replicated, may hold values from -0.25 to 0.25
- sketch_right: bfloat16 [512, 64], P('rep'), may hold values from -0.25 to 0.25
- near_cols: int32 [48, 4], P('leaf'), may hold values from 0 to 47, as said below
- far_cols: int32 [48, 4], P('leaf'), may hold values from 0 to 47, as said below
- near_owner: int32 [48, 4], P('leaf'), may hold values from 0 to 7, as said below
- far_owner: int32 [48, 4], P('leaf'), may hold values from 0 to 7, as said below
- far_rank: int32 [48, 4], P('leaf'), may hold values from 8 to 64
Outputs:
- near_tiles: bfloat16 [8, 8, 6, 512, 512], P('leaf', None, None, 'rep')
- far_factors: bfloat16 [8, 8, 6, 512, 128], P('leaf', None, None, 'rep')
The draws below stay inside these ranges and needn't reach their ends.
Inputs may be any that keep to these rules, and one draw needn't show every extreme that they name: `panel_dest`: A permutation: rows d * 3072 to (d + 1) * 3072 - 1 of the cluster-ordered array belong to index d of leaf; the panels held by one index of leaf have at most 480 positions in the rows of any one index, and every index receives exactly 3072. For row cluster c the column clusters lie between (c // 6 - 1) * 6 and (c // 6 + 2) * 6 - 1; near_cols[c, 0] = c. `far_cols`: for row cluster c the column clusters lie between (c // 6 - 1) * 6 and (c // 6 + 2) * 6 - 1. `near_owner`: the near blocks of the clusters of one index of leaf name any one owner at most 6 times. `far_owner`: the far blocks of the clusters of one index of leaf name any one owner at most 6 times.
All inputs are finite; a program needn't handle non-finite values.
Results may differ from the reference program's by a relative error of at most 0.013.
Values may be sent and summed in bfloat16 or wider, within the bound.
A program may use at most 128 MiB of HBM per device.

```python
import math
import jax
import jax.numpy as jnp
from jax import lax

CL = 512
M = 1024
K = 64
NEAR = 4
FAR = 4
C_DEV = 6
PANEL_DEV = 3072
PANELS = 24576
CLUSTERS = 48
CAPN = 6
CAPF = 6
N_LEAF = 8
N_REP = 4


def draw_panel_dest(key, part):
    per_peer = PANEL_DEV // N_LEAF
    spread = max(1, per_peer // 4)
    halfway = N_LEAF // 2
    flips = jnp.where(jax.random.permutation(jax.random.fold_in(key, 11), N_LEAF) < halfway, 1, -1).astype(jnp.int32)
    source = jnp.arange(N_LEAF, dtype=jnp.int32)[:, None]
    target = jnp.arange(N_LEAF, dtype=jnp.int32)[None, :]
    counts = per_peer + spread * flips[(target - source) % N_LEAF]
    ending = jnp.cumsum(counts, axis=1)
    starting = ending - counts
    arrivals = jnp.cumsum(counts, axis=0) - counts
    ranking = jax.vmap(lambda subkey: jax.random.permutation(subkey, PANEL_DEV))(jax.random.split(jax.random.fold_in(key, 12), N_LEAF)).astype(jnp.int32)
    owner_of = jnp.sum((ranking[:, :, None] >= ending[:, None, :]).astype(jnp.int32), axis=2)
    within = ranking - jnp.take_along_axis(starting, owner_of, axis=1)
    arrival = jnp.take_along_axis(arrivals, owner_of, axis=1) + within
    shuffles = jax.vmap(lambda subkey: jax.random.permutation(subkey, PANEL_DEV))(jax.random.split(jax.random.fold_in(key, 13), N_LEAF)).astype(jnp.int32)
    placed = shuffles[owner_of, arrival]
    return (owner_of * PANEL_DEV + placed).reshape(PANELS).astype(jnp.int32)


def column_pick(key, amount, sided):
    cluster = jnp.arange(CLUSTERS, dtype=jnp.int32)[:, None]
    holder = cluster // C_DEV
    lowest = jnp.maximum(holder - 1, 0) * C_DEV
    highest = jnp.minimum(holder + 2, N_LEAF) * C_DEV
    drawn = jax.random.randint(key, (CLUSTERS, amount), 0, 1 << 24)
    chosen = lowest + drawn % (highest - lowest)
    if sided:
        left_start = jnp.where(holder > 0, holder - 1, holder) * C_DEV
        right_start = jnp.where(holder < N_LEAF - 1, holder + 1, holder) * C_DEV
        chosen = chosen.at[:, 0].set((left_start + drawn[:, 0:1] % C_DEV)[:, 0])
        chosen = chosen.at[:, 1].set((right_start + drawn[:, 1:2] % C_DEV)[:, 0])
    else:
        chosen = chosen.at[:, 0].set(cluster[:, 0])
    return chosen.astype(jnp.int32)


def draw_near_cols(key, part):
    return column_pick(jax.random.fold_in(key, 21), NEAR, False)


def draw_far_cols(key, part):
    return column_pick(jax.random.fold_in(key, 22), FAR, True)


def owner_pick(key, per_cluster):
    blocks = C_DEV * per_cluster
    capacity = max(2, (2 * blocks + N_LEAF - 1) // N_LEAF)
    busiest = jax.random.randint(jax.random.fold_in(key, 1), (), 0, N_LEAF).astype(jnp.int32)
    serial = jnp.arange(blocks, dtype=jnp.int32)

    def for_source(subkey):
        others = jax.random.permutation(jax.random.fold_in(subkey, 2), N_LEAF - 1).astype(jnp.int32)
        others = others + (others >= busiest).astype(jnp.int32)
        assigned = jnp.where(serial < capacity, busiest, others[(serial - capacity) % (N_LEAF - 1)])
        return jax.random.permutation(jax.random.fold_in(subkey, 3), assigned)
    picked = jax.vmap(for_source)(jax.random.split(jax.random.fold_in(key, 4), N_LEAF))
    return picked.reshape(CLUSTERS, per_cluster).astype(jnp.int32)


def draw_near_owner(key, part):
    return owner_pick(jax.random.fold_in(key, 31), NEAR)


def draw_far_owner(key, part):
    return owner_pick(jax.random.fold_in(key, 32), FAR)


def plant(entries, own_key, smallest, high):
    longest = entries.shape.index(max(entries.shape))
    spots = []
    for shift in (0, 1):
        where = [jax.random.randint(jax.random.fold_in(own_key, axis), (), 0, length) for axis, length in enumerate(entries.shape)]
        where[longest] = (where[longest] + shift) % entries.shape[longest]
        spots.append(tuple(where))
    return entries.at[spots[0]].set(smallest).at[spots[1]].set(high)


def block_levels(rng, dims, cuts, smallest, high):
    level, own = 1.0, jax.random.fold_in(rng, 6)
    for position, shards_of in cuts:
        heights = jnp.exp(jax.random.uniform(jax.random.fold_in(own, position), (shards_of,), jnp.float32, smallest / len(cuts), high / len(cuts)))
        level = level * jnp.repeat(heights, dims[position] // shards_of).reshape([-1 if axis == position else 1 for axis in range(len(dims))])
    return level


def scatter_about(key, shape, scale, reach, cuts=(), held_as=jnp.bfloat16):
    values = scale * jax.random.normal(key, shape, jnp.float32)
    if cuts:
        values = values * block_levels(key, shape, cuts, -0.22, 0.18)
    return jnp.clip(values, -reach, reach).astype(held_as)


def setup_inputs(seed: int = 0) -> dict:
    keys = jax.random.split(jax.random.key(seed), 11)
    return {
        "panel_feats": scatter_about(keys[0], (PANELS, 2, M), 1.0, 6.0, ((0, 8), (2, 4))),
        "panel_dest": draw_panel_dest(jax.random.fold_in(keys[10], 71), 0),
        "coefs": jnp.clip(jax.random.uniform(keys[2], (M,), jnp.float32, -2.0, 2.0) * block_levels(keys[2], (M,), ((0, 4),), -0.4, 0.0), -2.0, 2.0),
        "sketch_left": scatter_about(keys[3], (CL, K), CL ** -0.5, 0.25),
        "sketch_right": scatter_about(keys[4], (CL, K), CL ** -0.5, 0.25, ((0, 4),)),
        "near_cols": draw_near_cols(jax.random.fold_in(keys[10], 71), 0),
        "far_cols": draw_far_cols(jax.random.fold_in(keys[10], 71), 0),
        "near_owner": draw_near_owner(jax.random.fold_in(keys[10], 71), 0),
        "far_owner": draw_far_owner(jax.random.fold_in(keys[10], 71), 0),
        "far_rank": plant(jax.random.randint(keys[9], (CLUSTERS, FAR), K // 8, K + 1), jax.random.fold_in(keys[9], 1), K // 8, K).astype(jnp.int32),
    }


def slot_places(owners, capacity):
    by_source = owners.reshape(N_LEAF, -1)
    onehot = (by_source[:, :, None] == jnp.arange(N_LEAF, dtype=jnp.int32)[None, None, :]).astype(jnp.int32)
    before = lax.optimization_barrier(jnp.sum(jnp.cumsum(onehot, axis=1) * onehot, axis=2)) - 1
    source = jnp.arange(N_LEAF, dtype=jnp.int32)[:, None]
    return ((by_source * N_LEAF + source) * capacity + before).reshape(-1).astype(jnp.int32)

def reference(panel_feats, panel_dest, coefs, sketch_left, sketch_right, near_cols, far_cols, near_owner, far_owner, far_rank):
    records = jnp.zeros_like(panel_feats).at[panel_dest].set(panel_feats)
    scaled = (records[:, 0, :].astype(jnp.float32) * coefs.astype(jnp.float32)).astype(jnp.bfloat16)
    scaled = scaled.reshape(CLUSTERS, CL, M)
    field_rows = records[:, 1, :].reshape(CLUSTERS, CL, M)
    columns = jnp.concatenate([near_cols, far_cols], axis=1)
    group_size = M // N_REP

    def cluster_tiles(cluster):
        row_block = scaled[cluster].reshape(CL, N_REP, group_size).astype(jnp.float32)
        picked = jnp.take(field_rows, columns[cluster], axis=0).reshape(NEAR + FAR, CL, N_REP, group_size).astype(jnp.float32)
        partials = jnp.einsum('rgd,jcgd->gjrc', row_block, picked)
        rounded = lax.optimization_barrier(partials.astype(jnp.bfloat16))
        summed = lax.optimization_barrier(jnp.sum(rounded.astype(jnp.float32), axis=0)) / math.sqrt(M)
        kernel = (summed * lax.rsqrt(1.0 + summed * summed)).astype(jnp.bfloat16)
        distant = kernel[NEAR:].astype(jnp.float32)
        left_factor = jnp.einsum('jrc,ck->jrk', distant, sketch_left.astype(jnp.float32))
        right_factor = jnp.einsum('jrc,rk->jck', distant, sketch_right.astype(jnp.float32))
        rank_mask = (jnp.arange(K, dtype=jnp.int32)[None, :] < far_rank[cluster][:, None]).astype(jnp.float32)[:, None, :]
        factor = jnp.concatenate([left_factor * rank_mask, right_factor * rank_mask], axis=-1).astype(jnp.bfloat16)
        return (kernel[:NEAR], factor)
    near_all, far_all = lax.map(cluster_tiles, jnp.arange(CLUSTERS, dtype=jnp.int32))
    near_slots = slot_places(near_owner, CAPN)
    far_slots = slot_places(far_owner, CAPF)
    near_tiles = jnp.zeros((N_LEAF * N_LEAF * CAPN, CL, CL), near_all.dtype).at[near_slots].set(near_all.reshape(-1, CL, CL))
    far_factors = jnp.zeros((N_LEAF * N_LEAF * CAPF, CL, 2 * K), far_all.dtype).at[far_slots].set(far_all.reshape(-1, CL, 2 * K))
    return (near_tiles.reshape(N_LEAF, N_LEAF, CAPN, CL, CL), far_factors.reshape(N_LEAF, N_LEAF, CAPF, CL, 2 * K))
```

```python
import functools
import math

import jax
import jax.numpy as jnp
from jax import lax
from jax.experimental import pallas as pl
from jax.experimental.pallas import tpu as pltpu
from jax.sharding import PartitionSpec as P

VMEM_LIMIT = 56 * 1024 * 1024


def ranks(owners, leaf_count):
    onehot = (owners[:, None] == jnp.arange(leaf_count, dtype=jnp.int32)[None, :]).astype(jnp.int32)
    return jnp.sum(jnp.cumsum(onehot, axis=0) * onehot, axis=1) - 1


def block_of_slot(owners, capacity, leaf_count):
    slots = owners * capacity + ranks(owners, leaf_count)
    hits = jnp.arange(leaf_count * capacity, dtype=jnp.int32)[:, None] == slots[None, :]
    sources = jnp.arange(owners.shape[0], dtype=jnp.int32)[None, :]
    return jnp.max(jnp.where(hits, sources, -1), axis=1)


def tile(scaled_ref, cluster, fields_ref, column, scale):
    total = None
    for group in range(scaled_ref.shape[0]):
        term = lax.dot_general(
            scaled_ref[group, cluster],
            fields_ref[column // scaled_ref.shape[1], group, column % scaled_ref.shape[1]],
            (((1,), (1,)), ((), ())),
            preferred_element_type=jnp.float32,
        )
        total = term if total is None else total + term
    summed = total * scale
    return (summed * lax.rsqrt(1.0 + summed * summed)).astype(jnp.bfloat16)


def load_fields(sides, fields, sems):
    copies = [pltpu.make_async_copy(side, fields.at[i], sems.at[i]) for i, side in enumerate(sides)]
    for copy in copies:
        copy.start()
    for copy in copies:
        copy.wait()


def near_kernel(
    scale, cap, pick, cluster, column, scaled, left, own, right, out, fields, sems
):
    step = pl.program_id(0)

    @pl.when(step == 0)
    def _():
        load_fields((left, own, right), fields, sems)

    for slot in range(cap):
        n = step * cap + slot

        @pl.when(pick[n] >= 0)
        def _():
            made = tile(scaled, cluster[n], fields, column[n], scale)
            share = out.shape[3]
            for r in range(out.shape[1]):
                out[0, r, slot] = made[r * share : (r + 1) * share]

        @pl.when(pick[n] < 0)
        def _():
            out[0, :, slot] = jnp.zeros((out.shape[1],) + out.shape[3:], out.dtype)


def far_kernel(
    scale, column, scaled, left, own, right, sk_left, sk_right, left_out, right_out, fields, sems
):
    step = pl.program_id(0)

    @pl.when(step == 0)
    def _():
        load_fields((left, own, right), fields, sems)

    count = right_out.shape[1]
    for f in range(count):
        made = tile(scaled, step, fields, column[step * count + f], scale)
        right_out[0, f] = lax.dot_general(
            made, sk_right[...], (((0,), (0,)), ((), ())), preferred_element_type=jnp.float32
        )
        part = jnp.dot(made, sk_left[...], preferred_element_type=jnp.float32).astype(jnp.bfloat16)
        share = made.shape[0] // left_out.shape[0]
        half = share // 2
        for r in range(left_out.shape[0]):
            base = r * share
            left_out[r, 0, f] = jnp.concatenate(
                [part[base : base + half], part[base + half : base + share]], axis=1
            )


def join_kernel(cap, pick, rank, got_left, right, out):
    step = pl.program_id(0)
    for slot in range(cap):
        n = step * cap + slot

        @pl.when(pick[n] >= 0)
        def _():
            block = pick[n]
            total = got_left[0, block].astype(jnp.float32)
            for r in range(1, got_left.shape[0]):
                total = total + got_left[r, block].astype(jnp.float32)
            width = total.shape[1] // 2
            left = jnp.concatenate([total[:, :width], total[:, width:]], axis=0)
            both = jnp.concatenate([left, right[block]], axis=1)
            column = lax.broadcasted_iota(jnp.int32, both.shape, 1) % width
            out[0, slot] = jnp.where(column < rank[n], both, 0.0).astype(out.dtype)

        @pl.when(pick[n] < 0)
        def _():
            out[0, slot] = jnp.zeros(out.shape[2:], out.dtype)


def local(
    panel_feats,
    panel_dest,
    coefs,
    sketch_left,
    sketch_right,
    near_cols,
    far_cols,
    near_owner,
    far_owner,
    far_rank,
):
    bf16, f32 = jnp.bfloat16, jnp.float32
    leaf_count = lax.axis_size("leaf")
    groups = lax.axis_size("rep")
    position = lax.axis_index("leaf")
    panel_rows = panel_feats.shape[0]
    terms = panel_feats.shape[2]
    clusters = near_cols.shape[0]
    near_count = near_cols.shape[1]
    far_count = far_cols.shape[1]
    size = panel_rows // clusters
    share = size // groups
    width = sketch_left.shape[1]
    per_peer = panel_rows // leaf_count
    capacity = per_peer + max(1, per_peer // 4)
    slot_total = leaf_count * capacity
    near_cap = max(2, (2 * clusters * near_count + leaf_count - 1) // leaf_count)
    far_cap = max(2, (2 * clusters * far_count + leaf_count - 1) // leaf_count)
    scale = 1.0 / math.sqrt(terms * groups)

    def exchange(x, axis):
        return lax.all_to_all(x, axis, split_axis=0, concat_axis=0, tiled=True)

    dest_owner = panel_dest // panel_rows
    place = panel_dest % panel_rows
    outgoing = dest_owner * capacity + ranks(dest_owner, leaf_count)
    pack = (jnp.arange(slot_total, dtype=jnp.int32)[:, None] == outgoing[None, :]).astype(bf16)
    codes = jnp.stack([place // 128, place % 128, jnp.ones_like(place)], axis=1).astype(bf16)
    sent = jnp.dot(pack, codes, preferred_element_type=f32).astype(jnp.int32)
    send_place = jnp.where(sent[:, 2] > 0, sent[:, 0] * 128 + sent[:, 1], panel_rows)
    got_place = exchange(send_place.reshape(leaf_count, capacity), "leaf").reshape(-1)

    def moved(feats):
        packed = jnp.dot(pack, feats, preferred_element_type=f32).astype(bf16)
        return exchange(packed.reshape(leaf_count, capacity, terms), "leaf").reshape(slot_total, terms)

    got_field = moved(panel_feats[:, 1, :])
    got_source = moved(panel_feats[:, 0, :])
    row = jnp.arange(panel_rows, dtype=jnp.int32)
    by_share = row.reshape(clusters, groups, share).transpose(1, 0, 2).reshape(-1)
    sort_share = (by_share[:, None] == got_place[None, :]).astype(bf16)
    field = jnp.dot(sort_share, got_field, preferred_element_type=f32).astype(bf16)
    own = exchange(field.reshape(groups, clusters, share, terms), "rep")
    ends = leaf_count - 1
    left = lax.ppermute(own, "leaf", [(i, i + 1) for i in range(ends)])
    right = lax.ppermute(own, "leaf", [(i + 1, i) for i in range(ends)])
    sort = (row[:, None] == got_place[None, :]).astype(bf16)
    source = jnp.dot(sort, got_source, preferred_element_type=f32)
    scaled = (source.astype(bf16).astype(f32) * coefs).astype(bf16)
    scaled = lax.all_gather(scaled.reshape(clusters, size, terms), "rep")

    near_column = (near_cols - (position - 1) * clusters).reshape(-1)
    far_column = (far_cols - (position - 1) * clusters).reshape(-1)
    near_pick = block_of_slot(near_owner.reshape(-1), near_cap, leaf_count)
    far_pick = block_of_slot(far_owner.reshape(-1), far_cap, leaf_count)
    near_at = jnp.maximum(near_pick, 0)
    far_at = jnp.maximum(far_pick, 0)
    any_spec = pl.BlockSpec(memory_space=pl.ANY)
    scratch = [
        pltpu.VMEM((3, groups, clusters, share, terms), bf16),
        pltpu.SemaphoreType.DMA((3,)),
    ]
    params = pltpu.CompilerParams(vmem_limit_bytes=VMEM_LIMIT)
    whole = lambda *_: (0, 0, 0, 0)
    near_flops = 2 * clusters * near_count * size * share * terms * groups

    near_send = pl.pallas_call(
        functools.partial(near_kernel, scale, near_cap),
        out_shape=jax.ShapeDtypeStruct((leaf_count, groups, near_cap, share, share), bf16),
        grid_spec=pltpu.PrefetchScalarGridSpec(
            num_scalar_prefetch=3,
            grid=(leaf_count,),
            in_specs=[
                pl.BlockSpec(
                    (groups, clusters, size, terms), whole, pipeline_mode=pl.Buffered(1)
                ),
                any_spec,
                any_spec,
                any_spec,
            ],
            out_specs=pl.BlockSpec(
                (1, groups, near_cap, share, share), lambda i, *_: (i, 0, 0, 0, 0)
            ),
            scratch_shapes=scratch,
        ),
        compiler_params=params,
        cost_estimate=pl.CostEstimate(
            flops=near_flops, bytes_accessed=18 * 1024 * 1024, transcendentals=0
        ),
        name="near",
    )(near_pick, near_at // near_count, near_column[near_at], scaled, left, own, right)

    got_near = exchange(
        near_send.reshape(leaf_count * groups, near_cap, share, share), ("leaf", "rep")
    )
    near_out = (
        got_near.reshape(leaf_count, groups, near_cap, share, share)
        .transpose(0, 2, 3, 1, 4)
        .reshape(leaf_count, near_cap, share, size)
    )

    all_right = lax.all_gather(sketch_right, "rep", tiled=True)
    my_left = lax.dynamic_slice_in_dim(sketch_left, lax.axis_index("rep") * share, share, axis=0)
    left_parts, right_rows = pl.pallas_call(
        functools.partial(far_kernel, scale),
        out_shape=(
            jax.ShapeDtypeStruct((groups, clusters, far_count, share // 2, 2 * width), bf16),
            jax.ShapeDtypeStruct((clusters, far_count, share, width), f32),
        ),
        grid_spec=pltpu.PrefetchScalarGridSpec(
            num_scalar_prefetch=1,
            grid=(clusters,),
            in_specs=[
                pl.BlockSpec(
                    (groups, clusters, size, terms), whole, pipeline_mode=pl.Buffered(1)
                ),
                any_spec,
                any_spec,
                any_spec,
                pl.BlockSpec((share, width), lambda *_: (0, 0)),
                pl.BlockSpec((size, width), lambda *_: (0, 0)),
            ],
            out_specs=(
                pl.BlockSpec(
                    (groups, 1, far_count, share // 2, 2 * width), lambda i, *_: (0, i, 0, 0, 0)
                ),
                pl.BlockSpec((1, far_count, share, width), lambda i, *_: (i, 0, 0, 0)),
            ),
            scratch_shapes=scratch,
        ),
        compiler_params=params,
        cost_estimate=pl.CostEstimate(
            flops=near_flops, bytes_accessed=16 * 1024 * 1024, transcendentals=0
        ),
        name="far",
    )(far_column, scaled, left, own, right, my_left, all_right)

    blocks = clusters * far_count
    got_left = exchange(left_parts, "rep").reshape(groups, blocks, share // 2, 2 * width)
    far_send = pl.pallas_call(
        functools.partial(join_kernel, far_cap),
        out_shape=jax.ShapeDtypeStruct((leaf_count, far_cap, share, 2 * width), bf16),
        grid_spec=pltpu.PrefetchScalarGridSpec(
            num_scalar_prefetch=2,
            grid=(leaf_count,),
            in_specs=[
                pl.BlockSpec((groups, blocks, share // 2, 2 * width), whole),
                pl.BlockSpec((blocks, share, width), lambda *_: (0, 0, 0)),
            ],
            out_specs=pl.BlockSpec((1, far_cap, share, 2 * width), lambda i, *_: (i, 0, 0, 0)),
        ),
        compiler_params=params,
        cost_estimate=pl.CostEstimate(
            flops=1 << 20, bytes_accessed=4 * 1024 * 1024, transcendentals=0
        ),
        name="join",
    )(
        far_pick,
        far_rank.reshape(-1)[far_at],
        got_left,
        right_rows.reshape(blocks, share, width),
    )
    got_far = exchange(far_send, "leaf")
    return (near_out[None], got_far[None])


def solution(mesh):
    in_specs = (
        P("leaf", None, "rep"),
        P("leaf"),
        P("rep"),
        P(),
        P("rep", None),
        P("leaf", None),
        P("leaf", None),
        P("leaf", None),
        P("leaf", None),
        P("leaf", None),
    )
    out_specs = (P("leaf", None, None, "rep", None), P("leaf", None, None, "rep", None))
    return jax.shard_map(local, mesh=mesh, in_specs=in_specs, out_specs=out_specs, check_vma=False)
```

```python
import functools
import math

import jax
import jax.numpy as jnp
from jax import lax
from jax.experimental import pallas as pl
from jax.experimental.pallas import tpu as pltpu
from jax.sharding import PartitionSpec as P

VMEM_LIMIT = 56 * 1024 * 1024


def ranks(owners, leaf_count):
    onehot = (owners[:, None] == jnp.arange(leaf_count, dtype=jnp.int32)[None, :]).astype(jnp.int32)
    return jnp.sum(jnp.cumsum(onehot, axis=0) * onehot, axis=1) - 1


def block_of_slot(owners, capacity, leaf_count):
    slots = owners * capacity + ranks(owners, leaf_count)
    hits = jnp.arange(leaf_count * capacity, dtype=jnp.int32)[:, None] == slots[None, :]
    sources = jnp.arange(owners.shape[0], dtype=jnp.int32)[None, :]
    return jnp.max(jnp.where(hits, sources, -1), axis=1)


def tile(scaled_ref, cluster, fields_ref, column, scale):
    total = None
    for group in range(scaled_ref.shape[0]):
        term = lax.dot_general(
            scaled_ref[group, cluster],
            fields_ref[column // scaled_ref.shape[1], group, column % scaled_ref.shape[1]],
            (((1,), (1,)), ((), ())),
            preferred_element_type=jnp.float32,
        )
        total = term if total is None else total + term
    summed = total * scale
    return (summed * lax.rsqrt(1.0 + summed * summed)).astype(jnp.bfloat16)


def load_fields(sides, fields, sems):
    copies = [pltpu.make_async_copy(side, fields.at[i], sems.at[i]) for i, side in enumerate(sides)]
    for copy in copies:
        copy.start()
    for copy in copies:
        copy.wait()


def near_kernel(
    scale, cap, pick, cluster, column, scaled, left, own, right, out, fields, sems
):
    step = pl.program_id(0)

    @pl.when(step == 0)
    def _():
        load_fields((left, own, right), fields, sems)

    for slot in range(cap):
        n = step * cap + slot

        @pl.when(pick[n] >= 0)
        def _():
            made = tile(scaled, cluster[n], fields, column[n], scale)
            share = out.shape[3]
            for r in range(out.shape[1]):
                out[0, r, slot] = made[r * share : (r + 1) * share]

        @pl.when(pick[n] < 0)
        def _():
            out[0, :, slot] = jnp.zeros((out.shape[1],) + out.shape[3:], out.dtype)


def far_kernel(
    scale, column, scaled, left, own, right, sk_left, sk_right, left_out, right_out, fields, sems
):
    step = pl.program_id(0)

    @pl.when(step == 0)
    def _():
        load_fields((left, own, right), fields, sems)

    count = right_out.shape[1]
    for f in range(count):
        made = tile(scaled, step, fields, column[step * count + f], scale)
        right_out[0, f] = lax.dot_general(
            made, sk_right[...], (((0,), (0,)), ((), ())), preferred_element_type=jnp.float32
        )
        part = jnp.dot(made, sk_left[...], preferred_element_type=jnp.float32).astype(jnp.bfloat16)
        share = made.shape[0] // left_out.shape[0]
        half = share // 2
        for r in range(left_out.shape[0]):
            base = r * share
            left_out[r, 0, f] = jnp.concatenate(
                [part[base : base + half], part[base + half : base + share]], axis=1
            )


def join_kernel(cap, pick, rank, left_rows, right, out):
    step = pl.program_id(0)
    for slot in range(cap):
        n = step * cap + slot

        @pl.when(pick[n] >= 0)
        def _():
            block = pick[n]
            total = left_rows[block].astype(jnp.float32)
            width = total.shape[1] // 2
            left = jnp.concatenate([total[:, :width], total[:, width:]], axis=0)
            both = jnp.concatenate([left, right[block]], axis=1)
            column = lax.broadcasted_iota(jnp.int32, both.shape, 1) % width
            out[0, slot] = jnp.where(column < rank[n], both, 0.0).astype(out.dtype)

        @pl.when(pick[n] < 0)
        def _():
            out[0, slot] = jnp.zeros(out.shape[2:], out.dtype)


def join_columns(got, out):
    share = got.shape[4]
    for r in range(got.shape[1]):
        out[0, 0, :, :, r * share : (r + 1) * share] = got[0, r]


def local(
    panel_feats,
    panel_dest,
    coefs,
    sketch_left,
    sketch_right,
    near_cols,
    far_cols,
    near_owner,
    far_owner,
    far_rank,
):
    bf16, f32 = jnp.bfloat16, jnp.float32
    leaf_count = lax.axis_size("leaf")
    groups = lax.axis_size("rep")
    position = lax.axis_index("leaf")
    panel_rows = panel_feats.shape[0]
    terms = panel_feats.shape[2]
    clusters = near_cols.shape[0]
    near_count = near_cols.shape[1]
    far_count = far_cols.shape[1]
    size = panel_rows // clusters
    share = size // groups
    width = sketch_left.shape[1]
    per_peer = panel_rows // leaf_count
    capacity = per_peer + max(1, per_peer // 4)
    slot_total = leaf_count * capacity
    near_cap = max(2, (2 * clusters * near_count + leaf_count - 1) // leaf_count)
    far_cap = max(2, (2 * clusters * far_count + leaf_count - 1) // leaf_count)
    scale = 1.0 / math.sqrt(terms * groups)

    def exchange(x, axis):
        return lax.all_to_all(x, axis, split_axis=0, concat_axis=0, tiled=True)

    dest_owner = panel_dest // panel_rows
    place = panel_dest % panel_rows
    outgoing = dest_owner * capacity + ranks(dest_owner, leaf_count)
    pack = (jnp.arange(slot_total, dtype=jnp.int32)[:, None] == outgoing[None, :]).astype(bf16)
    codes = jnp.stack([place // 128, place % 128, jnp.ones_like(place)], axis=1).astype(bf16)
    sent = jnp.dot(pack, codes, preferred_element_type=f32).astype(jnp.int32)
    send_place = jnp.where(sent[:, 2] > 0, sent[:, 0] * 128 + sent[:, 1], panel_rows)
    got_place = exchange(send_place.reshape(leaf_count, capacity), "leaf").reshape(-1)

    def packed(feats):
        rows = jnp.dot(pack, feats, preferred_element_type=f32).astype(bf16)
        return rows.reshape(leaf_count, capacity, terms)

    got_field = exchange(packed(panel_feats[:, 1, :]), "leaf")
    send_source, got_field = lax.optimization_barrier((packed(panel_feats[:, 0, :]), got_field))
    got_field = got_field.reshape(slot_total, terms)
    got_source = exchange(send_source, "leaf").reshape(slot_total, terms)
    row = jnp.arange(panel_rows, dtype=jnp.int32)
    by_share = row.reshape(clusters, groups, share).transpose(1, 0, 2).reshape(-1)
    sort_share = (by_share[:, None] == got_place[None, :]).astype(bf16)
    field = jnp.dot(sort_share, got_field, preferred_element_type=f32).astype(bf16)
    own = exchange(field.reshape(groups, clusters, share, terms), "rep")
    ends = leaf_count - 1
    left = lax.ppermute(own, "leaf", [(i, i + 1) for i in range(ends)])
    right = lax.ppermute(own, "leaf", [(i + 1, i) for i in range(ends)])
    sort = (row[:, None] == got_place[None, :]).astype(bf16)
    source = jnp.dot(sort, got_source, preferred_element_type=f32)
    scaled = (source.astype(bf16).astype(f32) * coefs).astype(bf16)
    scaled = lax.all_gather(scaled.reshape(clusters, size, terms), "rep")

    near_column = (near_cols - (position - 1) * clusters).reshape(-1)
    far_column = (far_cols - (position - 1) * clusters).reshape(-1)
    near_pick = block_of_slot(near_owner.reshape(-1), near_cap, leaf_count)
    far_pick = block_of_slot(far_owner.reshape(-1), far_cap, leaf_count)
    near_at = jnp.maximum(near_pick, 0)
    far_at = jnp.maximum(far_pick, 0)
    any_spec = pl.BlockSpec(memory_space=pl.ANY)
    scratch = [
        pltpu.VMEM((3, groups, clusters, share, terms), bf16),
        pltpu.SemaphoreType.DMA((3,)),
    ]
    params = pltpu.CompilerParams(vmem_limit_bytes=VMEM_LIMIT)
    whole = lambda *_: (0, 0, 0, 0)
    near_flops = 2 * clusters * near_count * size * share * terms * groups

    near_send = pl.pallas_call(
        functools.partial(near_kernel, scale, near_cap),
        out_shape=jax.ShapeDtypeStruct((leaf_count, groups, near_cap, share, share), bf16),
        grid_spec=pltpu.PrefetchScalarGridSpec(
            num_scalar_prefetch=3,
            grid=(leaf_count,),
            in_specs=[
                pl.BlockSpec(
                    (groups, clusters, size, terms), whole, pipeline_mode=pl.Buffered(1)
                ),
                any_spec,
                any_spec,
                any_spec,
            ],
            out_specs=pl.BlockSpec(
                (1, groups, near_cap, share, share), lambda i, *_: (i, 0, 0, 0, 0)
            ),
            scratch_shapes=scratch,
        ),
        compiler_params=params,
        cost_estimate=pl.CostEstimate(
            flops=near_flops, bytes_accessed=18 * 1024 * 1024, transcendentals=0
        ),
        name="near",
    )(near_pick, near_at // near_count, near_column[near_at], scaled, left, own, right)

    near_send, far_scaled = lax.optimization_barrier((near_send, scaled))
    got_near = exchange(
        near_send.reshape(leaf_count * groups, near_cap, share, share), ("leaf", "rep")
    ).reshape(leaf_count, groups, near_cap, share, share)

    all_right = lax.all_gather(sketch_right, "rep", tiled=True)
    my_left = lax.dynamic_slice_in_dim(sketch_left, lax.axis_index("rep") * share, share, axis=0)
    left_parts, right_rows = pl.pallas_call(
        functools.partial(far_kernel, scale),
        out_shape=(
            jax.ShapeDtypeStruct((groups, clusters, far_count, share // 2, 2 * width), bf16),
            jax.ShapeDtypeStruct((clusters, far_count, share, width), f32),
        ),
        grid_spec=pltpu.PrefetchScalarGridSpec(
            num_scalar_prefetch=1,
            grid=(clusters,),
            in_specs=[
                pl.BlockSpec(
                    (groups, clusters, size, terms), whole, pipeline_mode=pl.Buffered(1)
                ),
                any_spec,
                any_spec,
                any_spec,
                pl.BlockSpec((share, width), lambda *_: (0, 0)),
                pl.BlockSpec((size, width), lambda *_: (0, 0)),
            ],
            out_specs=(
                pl.BlockSpec(
                    (groups, 1, far_count, share // 2, 2 * width), lambda i, *_: (0, i, 0, 0, 0)
                ),
                pl.BlockSpec((1, far_count, share, width), lambda i, *_: (i, 0, 0, 0)),
            ),
            scratch_shapes=scratch,
        ),
        compiler_params=params,
        cost_estimate=pl.CostEstimate(
            flops=near_flops, bytes_accessed=16 * 1024 * 1024, transcendentals=0
        ),
        name="far",
    )(far_column, far_scaled, left, own, right, my_left, all_right)

    blocks = clusters * far_count
    left_rows = lax.psum_scatter(left_parts, "rep", scatter_dimension=0, tiled=True)
    far_send = pl.pallas_call(
        functools.partial(join_kernel, far_cap),
        out_shape=jax.ShapeDtypeStruct((leaf_count, far_cap, share, 2 * width), bf16),
        grid_spec=pltpu.PrefetchScalarGridSpec(
            num_scalar_prefetch=2,
            grid=(leaf_count,),
            in_specs=[
                pl.BlockSpec((blocks, share // 2, 2 * width), lambda *_: (0, 0, 0)),
                pl.BlockSpec((blocks, share, width), lambda *_: (0, 0, 0)),
            ],
            out_specs=pl.BlockSpec((1, far_cap, share, 2 * width), lambda i, *_: (i, 0, 0, 0)),
        ),
        compiler_params=params,
        cost_estimate=pl.CostEstimate(
            flops=1 << 20, bytes_accessed=4 * 1024 * 1024, transcendentals=0
        ),
        name="join",
    )(
        far_pick,
        far_rank.reshape(-1)[far_at],
        left_rows.reshape(blocks, share // 2, 2 * width),
        right_rows.reshape(blocks, share, width),
    )
    far_send, got_near = lax.optimization_barrier((far_send, got_near))
    got_far = exchange(far_send, "leaf")
    near_out = pl.pallas_call(
        join_columns,
        out_shape=jax.ShapeDtypeStruct((1, leaf_count, near_cap, share, size), bf16),
        grid=(leaf_count,),
        in_specs=[
            pl.BlockSpec((1, groups, near_cap, share, share), lambda i: (i, 0, 0, 0, 0))
        ],
        out_specs=pl.BlockSpec((1, 1, near_cap, share, size), lambda i: (0, i, 0, 0, 0)),
        compiler_params=params,
        cost_estimate=pl.CostEstimate(
            flops=1 << 20, bytes_accessed=12 * 1024 * 1024, transcendentals=0
        ),
        name="columns",
    )(got_near)
    return (near_out, got_far[None])


def solution(mesh):
    in_specs = (
        P("leaf", None, "rep"),
        P("leaf"),
        P("rep"),
        P(),
        P("rep", None),
        P("leaf", None),
        P("leaf", None),
        P("leaf", None),
        P("leaf", None),
        P("leaf", None),
    )
    out_specs = (P("leaf", None, None, "rep", None), P("leaf", None, None, "rep", None))
    return jax.shard_map(local, mesh=mesh, in_specs=in_specs, out_specs=out_specs, check_vma=False)
```

```python
import functools
import math

import jax
import jax.numpy as jnp
from jax import lax
from jax.experimental import pallas as pl
from jax.experimental.pallas import tpu as pltpu
from jax.sharding import PartitionSpec as P

VMEM_LIMIT = 56 * 1024 * 1024


def ranks(owners, leaf_count):
    onehot = (owners[:, None] == jnp.arange(leaf_count, dtype=jnp.int32)[None, :]).astype(jnp.int32)
    return jnp.sum(jnp.cumsum(onehot, axis=0) * onehot, axis=1) - 1


def block_of_slot(owners, capacity, leaf_count):
    slots = owners * capacity + ranks(owners, leaf_count)
    hits = jnp.arange(leaf_count * capacity, dtype=jnp.int32)[:, None] == slots[None, :]
    sources = jnp.arange(owners.shape[0], dtype=jnp.int32)[None, :]
    return jnp.max(jnp.where(hits, sources, -1), axis=1)


def tile(order, scaled_ref, cluster, fields_ref, column, scale):
    total = None
    for group in range(scaled_ref.shape[0]):
        term = lax.dot_general(
            scaled_ref[order[group], cluster],
            fields_ref[column // scaled_ref.shape[1], group, column % scaled_ref.shape[1]],
            (((1,), (1,)), ((), ())),
            preferred_element_type=jnp.float32,
        )
        total = term if total is None else total + term
    summed = total * scale
    return (summed * lax.rsqrt(1.0 + summed * summed)).astype(jnp.bfloat16)


def load_fields(parts, fields, sems):
    copies = []
    for i, part in enumerate(parts):
        if i % 2 == 0:
            target = fields.at[i // 2, 0]
        else:
            target = fields.at[i // 2, pl.ds(1, fields.shape[1] - 1)]
        copies.append(pltpu.make_async_copy(part, target, sems.at[i]))
    for copy in copies:
        copy.start()
    for copy in copies:
        copy.wait()


def near_kernel(scale, cap, pick, cluster, column, order, scaled, *refs):
    parts, (out, fields, sems) = refs[:6], refs[6:]
    step = pl.program_id(0)

    @pl.when(step == 0)
    def _():
        load_fields(parts, fields, sems)

    for slot in range(cap):
        n = step * cap + slot

        @pl.when(pick[n] >= 0)
        def _():
            made = tile(order, scaled, cluster[n], fields, column[n], scale)
            share = out.shape[3]
            for r in range(out.shape[1]):
                out[0, r, slot] = made[r * share : (r + 1) * share]

        @pl.when(pick[n] < 0)
        def _():
            out[0, :, slot] = jnp.zeros((out.shape[1],) + out.shape[3:], out.dtype)


def far_kernel(scale, column, order, scaled, *refs):
    parts, (sk_left, sk_right, left_out, right_out, fields, sems) = refs[:6], refs[6:]
    step = pl.program_id(0)

    @pl.when(step == 0)
    def _():
        load_fields(parts, fields, sems)

    count = right_out.shape[1]
    for f in range(count):
        made = tile(order, scaled, step, fields, column[step * count + f], scale)
        right_out[0, f] = lax.dot_general(
            made, sk_right[...], (((0,), (0,)), ((), ())), preferred_element_type=jnp.float32
        )
        part = jnp.dot(made, sk_left[...], preferred_element_type=jnp.float32).astype(jnp.bfloat16)
        share = made.shape[0] // left_out.shape[0]
        half = share // 2
        for r in range(left_out.shape[0]):
            base = r * share
            left_out[r, 0, f] = jnp.concatenate(
                [part[base : base + half], part[base + half : base + share]], axis=1
            )


def join_kernel(cap, pick, rank, left_rows, right, out):
    step = pl.program_id(0)
    for slot in range(cap):
        n = step * cap + slot

        @pl.when(pick[n] >= 0)
        def _():
            block = pick[n]
            total = left_rows[block].astype(jnp.float32)
            width = total.shape[1] // 2
            left = jnp.concatenate([total[:, :width], total[:, width:]], axis=0)
            both = jnp.concatenate([left, right[block]], axis=1)
            column = lax.broadcasted_iota(jnp.int32, both.shape, 1) % width
            out[0, slot] = jnp.where(column < rank[n], both, 0.0).astype(out.dtype)

        @pl.when(pick[n] < 0)
        def _():
            out[0, slot] = jnp.zeros(out.shape[2:], out.dtype)


def join_columns(got, out):
    share = got.shape[4]
    for r in range(got.shape[1]):
        out[0, 0, :, :, r * share : (r + 1) * share] = got[0, r]


def local(
    panel_feats,
    panel_dest,
    coefs,
    sketch_left,
    sketch_right,
    near_cols,
    far_cols,
    near_owner,
    far_owner,
    far_rank,
):
    bf16, f32 = jnp.bfloat16, jnp.float32
    leaf_count = lax.axis_size("leaf")
    groups = lax.axis_size("rep")
    position = lax.axis_index("leaf")
    panel_rows = panel_feats.shape[0]
    terms = panel_feats.shape[2]
    clusters = near_cols.shape[0]
    near_count = near_cols.shape[1]
    far_count = far_cols.shape[1]
    size = panel_rows // clusters
    share = size // groups
    width = sketch_left.shape[1]
    per_peer = panel_rows // leaf_count
    capacity = per_peer + max(1, per_peer // 4)
    slot_total = leaf_count * capacity
    near_cap = max(2, (2 * clusters * near_count + leaf_count - 1) // leaf_count)
    far_cap = max(2, (2 * clusters * far_count + leaf_count - 1) // leaf_count)
    scale = 1.0 / math.sqrt(terms * groups)

    def exchange(x, axis):
        return lax.all_to_all(x, axis, split_axis=0, concat_axis=0, tiled=True)

    dest_owner = panel_dest // panel_rows
    outgoing = dest_owner * capacity + ranks(dest_owner, leaf_count)
    pack = (jnp.arange(slot_total, dtype=jnp.int32)[:, None] == outgoing[None, :]).astype(bf16)

    def packed(feats):
        rows = jnp.dot(pack, feats, preferred_element_type=f32).astype(bf16)
        return rows.reshape(leaf_count, capacity, terms)

    all_dest = lax.all_gather(panel_dest, "leaf")
    all_right = lax.all_gather(sketch_right, "rep", tiled=True)
    mine = (all_dest // panel_rows == position).astype(jnp.int32)
    incoming = jnp.where(mine > 0, jnp.cumsum(mine, axis=1) - 1, -1)
    hits = incoming[:, None, :] == jnp.arange(capacity, dtype=jnp.int32)[None, :, None]
    got_place = jnp.max(jnp.where(hits, (all_dest % panel_rows)[:, None, :], -1), axis=2).reshape(-1)

    got_field = exchange(packed(panel_feats[:, 1, :]), "leaf")
    send_source, got_field = lax.optimization_barrier((packed(panel_feats[:, 0, :]), got_field))
    got_field = got_field.reshape(slot_total, terms)
    got_source = exchange(send_source, "leaf").reshape(slot_total, terms)
    me = lax.axis_index("rep")
    steps = jnp.arange(groups, dtype=jnp.int32)
    turned = (me + steps) % groups
    order = (me - steps + groups) % groups
    inner = jnp.arange(share, dtype=jnp.int32)
    by_share = (
        jnp.arange(clusters, dtype=jnp.int32)[None, :, None] * size
        + turned[:, None, None] * share
        + inner[None, None, :]
    ).reshape(-1)
    sort_share = (by_share[:, None] == got_place[None, :]).astype(bf16)
    field = jnp.dot(sort_share, got_field, preferred_element_type=f32).astype(bf16)
    field = field.reshape(groups, clusters, share, terms)
    first = field[0]
    rest = jnp.stack(
        [
            lax.ppermute(field[k], "rep", [(i, (i + k) % groups) for i in range(groups)])
            for k in range(1, groups)
        ]
    )
    rest, all_right, got_source = lax.optimization_barrier((rest, all_right, got_source))
    ends = leaf_count - 1
    up = [(i, i + 1) for i in range(ends)]
    down = [(i + 1, i) for i in range(ends)]
    fields = (
        lax.ppermute(first, "leaf", up),
        lax.ppermute(rest, "leaf", up),
        first,
        rest,
        lax.ppermute(first, "leaf", down),
        lax.ppermute(rest, "leaf", down),
    )
    row = jnp.arange(panel_rows, dtype=jnp.int32)
    sort = (row[:, None] == got_place[None, :]).astype(bf16)
    source = jnp.dot(sort, got_source, preferred_element_type=f32)
    scaled = (source.astype(bf16).astype(f32) * coefs).astype(bf16)
    scaled = lax.all_gather(scaled.reshape(clusters, size, terms), "rep")

    near_column = (near_cols - (position - 1) * clusters).reshape(-1)
    far_column = (far_cols - (position - 1) * clusters).reshape(-1)
    near_pick = block_of_slot(near_owner.reshape(-1), near_cap, leaf_count)
    far_pick = block_of_slot(far_owner.reshape(-1), far_cap, leaf_count)
    near_at = jnp.maximum(near_pick, 0)
    far_at = jnp.maximum(far_pick, 0)
    any_spec = pl.BlockSpec(memory_space=pl.ANY)
    scratch = [
        pltpu.VMEM((3, groups, clusters, share, terms), bf16),
        pltpu.SemaphoreType.DMA((6,)),
    ]
    params = pltpu.CompilerParams(vmem_limit_bytes=VMEM_LIMIT)
    whole = lambda *_: (0, 0, 0, 0)
    near_flops = 2 * clusters * near_count * size * share * terms * groups

    near_send = pl.pallas_call(
        functools.partial(near_kernel, scale, near_cap),
        out_shape=jax.ShapeDtypeStruct((leaf_count, groups, near_cap, share, share), bf16),
        grid_spec=pltpu.PrefetchScalarGridSpec(
            num_scalar_prefetch=4,
            grid=(leaf_count,),
            in_specs=[
                pl.BlockSpec(
                    (groups, clusters, size, terms), whole, pipeline_mode=pl.Buffered(1)
                ),
                *[any_spec] * 6,
            ],
            out_specs=pl.BlockSpec(
                (1, groups, near_cap, share, share), lambda i, *_: (i, 0, 0, 0, 0)
            ),
            scratch_shapes=scratch,
        ),
        compiler_params=params,
        cost_estimate=pl.CostEstimate(
            flops=near_flops, bytes_accessed=18 * 1024 * 1024, transcendentals=0
        ),
        name="near",
    )(near_pick, near_at // near_count, near_column[near_at], order, scaled, *fields)

    near_send, far_scaled = lax.optimization_barrier((near_send, scaled))
    got_near = exchange(
        near_send.reshape(leaf_count * groups, near_cap, share, share), ("leaf", "rep")
    ).reshape(leaf_count, groups, near_cap, share, share)

    my_left = lax.dynamic_slice_in_dim(sketch_left, lax.axis_index("rep") * share, share, axis=0)
    left_parts, right_rows = pl.pallas_call(
        functools.partial(far_kernel, scale),
        out_shape=(
            jax.ShapeDtypeStruct((groups, clusters, far_count, share // 2, 2 * width), bf16),
            jax.ShapeDtypeStruct((clusters, far_count, share, width), f32),
        ),
        grid_spec=pltpu.PrefetchScalarGridSpec(
            num_scalar_prefetch=2,
            grid=(clusters,),
            in_specs=[
                pl.BlockSpec(
                    (groups, clusters, size, terms), whole, pipeline_mode=pl.Buffered(1)
                ),
                *[any_spec] * 6,
                pl.BlockSpec((share, width), lambda *_: (0, 0)),
                pl.BlockSpec((size, width), lambda *_: (0, 0)),
            ],
            out_specs=(
                pl.BlockSpec(
                    (groups, 1, far_count, share // 2, 2 * width), lambda i, *_: (0, i, 0, 0, 0)
                ),
                pl.BlockSpec((1, far_count, share, width), lambda i, *_: (i, 0, 0, 0)),
            ),
            scratch_shapes=scratch,
        ),
        compiler_params=params,
        cost_estimate=pl.CostEstimate(
            flops=near_flops, bytes_accessed=16 * 1024 * 1024, transcendentals=0
        ),
        name="far",
    )(far_column, order, far_scaled, *fields, my_left, all_right)

    blocks = clusters * far_count
    left_rows = lax.psum_scatter(left_parts, "rep", scatter_dimension=0, tiled=True)
    far_send = pl.pallas_call(
        functools.partial(join_kernel, far_cap),
        out_shape=jax.ShapeDtypeStruct((leaf_count, far_cap, share, 2 * width), bf16),
        grid_spec=pltpu.PrefetchScalarGridSpec(
            num_scalar_prefetch=2,
            grid=(leaf_count,),
            in_specs=[
                pl.BlockSpec((blocks, share // 2, 2 * width), lambda *_: (0, 0, 0)),
                pl.BlockSpec((blocks, share, width), lambda *_: (0, 0, 0)),
            ],
            out_specs=pl.BlockSpec((1, far_cap, share, 2 * width), lambda i, *_: (i, 0, 0, 0)),
        ),
        compiler_params=params,
        cost_estimate=pl.CostEstimate(
            flops=1 << 20, bytes_accessed=4 * 1024 * 1024, transcendentals=0
        ),
        name="join",
    )(
        far_pick,
        far_rank.reshape(-1)[far_at],
        left_rows.reshape(blocks, share // 2, 2 * width),
        right_rows.reshape(blocks, share, width),
    )
    far_send, got_near = lax.optimization_barrier((far_send, got_near))
    got_far = exchange(far_send, "leaf")
    near_out = pl.pallas_call(
        join_columns,
        out_shape=jax.ShapeDtypeStruct((1, leaf_count, near_cap, share, size), bf16),
        grid=(leaf_count,),
        in_specs=[
            pl.BlockSpec((1, groups, near_cap, share, share), lambda i: (i, 0, 0, 0, 0))
        ],
        out_specs=pl.BlockSpec((1, 1, near_cap, share, size), lambda i: (0, i, 0, 0, 0)),
        compiler_params=params,
        cost_estimate=pl.CostEstimate(
            flops=1 << 20, bytes_accessed=12 * 1024 * 1024, transcendentals=0
        ),
        name="columns",
    )(got_near)
    return (near_out, got_far[None])


def solution(mesh):
    in_specs = (
        P("leaf", None, "rep"),
        P("leaf"),
        P("rep"),
        P(),
        P("rep", None),
        P("leaf", None),
        P("leaf", None),
        P("leaf", None),
        P("leaf", None),
        P("leaf", None),
    )
    out_specs = (P("leaf", None, None, "rep", None), P("leaf", None, None, "rep", None))
    return jax.shard_map(local, mesh=mesh, in_specs=in_specs, out_specs=out_specs, check_vma=False)
```

```python
import functools
import math

import jax
import jax.numpy as jnp
from jax import lax
from jax.experimental import pallas as pl
from jax.experimental.pallas import tpu as pltpu
from jax.sharding import PartitionSpec as P

VMEM_LIMIT = 56 * 1024 * 1024


def ranks(owners, leaf_count):
    onehot = (owners[:, None] == jnp.arange(leaf_count, dtype=jnp.int32)[None, :]).astype(jnp.int32)
    return jnp.sum(jnp.cumsum(onehot, axis=0) * onehot, axis=1) - 1


def block_of_slot(owners, capacity, leaf_count):
    slots = owners * capacity + ranks(owners, leaf_count)
    hits = jnp.arange(leaf_count * capacity, dtype=jnp.int32)[:, None] == slots[None, :]
    sources = jnp.arange(owners.shape[0], dtype=jnp.int32)[None, :]
    return jnp.max(jnp.where(hits, sources, -1), axis=1)


def tile(order, scaled_ref, cluster, fields_ref, column, scale):
    total = None
    for group in range(scaled_ref.shape[0]):
        term = lax.dot_general(
            scaled_ref[order[group], cluster],
            fields_ref[column // scaled_ref.shape[1], group, column % scaled_ref.shape[1]],
            (((1,), (1,)), ((), ())),
            preferred_element_type=jnp.float32,
        )
        total = term if total is None else total + term
    summed = total * scale
    return (summed * lax.rsqrt(1.0 + summed * summed)).astype(jnp.bfloat16)


def load_fields(parts, fields, sems):
    copies = []
    for i, part in enumerate(parts):
        if i % 2 == 0:
            target = fields.at[i // 2, 0]
        else:
            target = fields.at[i // 2, pl.ds(1, fields.shape[1] - 1)]
        copies.append(pltpu.make_async_copy(part, target, sems.at[i]))
    for copy in copies:
        copy.start()
    for copy in copies:
        copy.wait()


def near_kernel(scale, cap, pick, cluster, column, order, scaled, *refs):
    parts, (out, fields, sems) = refs[:6], refs[6:]
    step = pl.program_id(0)

    @pl.when(step == 0)
    def _():
        load_fields(parts, fields, sems)

    for slot in range(cap):
        n = step * cap + slot

        @pl.when(pick[n] >= 0)
        def _():
            made = tile(order, scaled, cluster[n], fields, column[n], scale)
            share = out.shape[3]
            for r in range(out.shape[1]):
                out[0, r, slot] = made[r * share : (r + 1) * share]

        @pl.when(pick[n] < 0)
        def _():
            out[0, :, slot] = jnp.zeros((out.shape[1],) + out.shape[3:], out.dtype)


def far_kernel(scale, column, order, scaled, *refs):
    parts, (sk_left, sk_right, left_out, right_out, fields, sems) = refs[:6], refs[6:]
    step = pl.program_id(0)

    @pl.when(step == 0)
    def _():
        load_fields(parts, fields, sems)

    count = right_out.shape[1]
    for f in range(count):
        made = tile(order, scaled, step, fields, column[step * count + f], scale)
        right_out[0, f] = lax.dot_general(
            made, sk_right[...], (((0,), (0,)), ((), ())), preferred_element_type=jnp.float32
        )
        part = jnp.dot(made, sk_left[...], preferred_element_type=jnp.float32).astype(jnp.bfloat16)
        share = made.shape[0] // left_out.shape[0]
        half = share // 2
        for r in range(left_out.shape[0]):
            base = r * share
            left_out[r, 0, f] = jnp.concatenate(
                [part[base : base + half], part[base + half : base + share]], axis=1
            )


def join_kernel(cap, pick, rank, left_rows, right, out):
    step = pl.program_id(0)
    for slot in range(cap):
        n = step * cap + slot

        @pl.when(pick[n] >= 0)
        def _():
            block = pick[n]
            total = left_rows[block].astype(jnp.float32)
            width = total.shape[1] // 2
            left = jnp.concatenate([total[:, :width], total[:, width:]], axis=0)
            both = jnp.concatenate([left, right[block]], axis=1)
            column = lax.broadcasted_iota(jnp.int32, both.shape, 1) % width
            out[0, slot] = jnp.where(column < rank[n], both, 0.0).astype(out.dtype)

        @pl.when(pick[n] < 0)
        def _():
            out[0, slot] = jnp.zeros(out.shape[2:], out.dtype)


def join_columns(got, out):
    share = got.shape[4]
    for r in range(got.shape[1]):
        out[0, 0, :, :, r * share : (r + 1) * share] = got[0, r]


def local(
    panel_feats,
    panel_dest,
    coefs,
    sketch_left,
    sketch_right,
    near_cols,
    far_cols,
    near_owner,
    far_owner,
    far_rank,
):
    bf16, f32 = jnp.bfloat16, jnp.float32
    leaf_count = lax.axis_size("leaf")
    groups = lax.axis_size("rep")
    position = lax.axis_index("leaf")
    panel_rows = panel_feats.shape[0]
    terms = panel_feats.shape[2]
    clusters = near_cols.shape[0]
    near_count = near_cols.shape[1]
    far_count = far_cols.shape[1]
    size = panel_rows // clusters
    share = size // groups
    width = sketch_left.shape[1]
    per_peer = panel_rows // leaf_count
    capacity = per_peer + max(1, per_peer // 4)
    slot_total = leaf_count * capacity
    near_cap = max(2, (2 * clusters * near_count + leaf_count - 1) // leaf_count)
    far_cap = max(2, (2 * clusters * far_count + leaf_count - 1) // leaf_count)
    scale = 1.0 / math.sqrt(terms * groups)

    def exchange(x, axis):
        return lax.all_to_all(x, axis, split_axis=0, concat_axis=0, tiled=True)

    dest_owner = panel_dest // panel_rows
    outgoing = dest_owner * capacity + ranks(dest_owner, leaf_count)
    pack = (jnp.arange(slot_total, dtype=jnp.int32)[:, None] == outgoing[None, :]).astype(bf16)

    def packed(feats):
        rows = jnp.dot(pack, feats, preferred_element_type=f32).astype(bf16)
        return rows.reshape(leaf_count, capacity, terms)

    all_dest = lax.all_gather(panel_dest, "leaf")
    mine = (all_dest // panel_rows == position).astype(jnp.int32)
    incoming = jnp.where(mine > 0, jnp.cumsum(mine, axis=1) - 1, -1)
    hits = incoming[:, None, :] == jnp.arange(capacity, dtype=jnp.int32)[None, :, None]
    got_place = jnp.max(jnp.where(hits, (all_dest % panel_rows)[:, None, :], -1), axis=2).reshape(-1)

    def after(value, earlier):
        return lax.optimization_barrier((value, earlier))[0]

    got_field = exchange(after(packed(panel_feats[:, 1, :]), all_dest), "leaf")
    send_source = after(packed(panel_feats[:, 0, :]), got_field)
    got_field = got_field.reshape(slot_total, terms)
    got_source = exchange(send_source, "leaf").reshape(slot_total, terms)
    me = lax.axis_index("rep")
    steps = jnp.arange(groups, dtype=jnp.int32)
    turned = (me + steps) % groups
    order = (me - steps + groups) % groups
    inner = jnp.arange(share, dtype=jnp.int32)
    by_share = (
        jnp.arange(clusters, dtype=jnp.int32)[None, :, None] * size
        + turned[:, None, None] * share
        + inner[None, None, :]
    ).reshape(-1)
    sort_share = (by_share[:, None] == got_place[None, :]).astype(bf16)
    field = jnp.dot(sort_share, got_field, preferred_element_type=f32).astype(bf16)
    field = field.reshape(groups, clusters, share, terms)
    first = field[0]
    rest = jnp.stack(
        [
            lax.ppermute(field[k], "rep", [(i, (i + k) % groups) for i in range(groups)])
            for k in range(1, groups)
        ]
    )
    ends = leaf_count - 1
    up = [(i, i + 1) for i in range(ends)]
    down = [(i + 1, i) for i in range(ends)]
    fields = (
        lax.ppermute(first, "leaf", up),
        lax.ppermute(rest, "leaf", up),
        first,
        rest,
        lax.ppermute(first, "leaf", down),
        lax.ppermute(rest, "leaf", down),
    )
    row = jnp.arange(panel_rows, dtype=jnp.int32)
    sort = (row[:, None] == after(got_place, rest)[None, :]).astype(bf16)
    source = jnp.dot(sort, got_source, preferred_element_type=f32)
    scaled = (source.astype(bf16).astype(f32) * coefs).astype(bf16)
    scaled = lax.all_gather(scaled.reshape(clusters, size, terms), "rep")

    near_column = (near_cols - (position - 1) * clusters).reshape(-1)
    far_column = (far_cols - (position - 1) * clusters).reshape(-1)
    near_pick = block_of_slot(near_owner.reshape(-1), near_cap, leaf_count)
    far_pick = block_of_slot(far_owner.reshape(-1), far_cap, leaf_count)
    near_at = jnp.maximum(near_pick, 0)
    far_at = jnp.maximum(far_pick, 0)
    any_spec = pl.BlockSpec(memory_space=pl.ANY)
    scratch = [
        pltpu.VMEM((3, groups, clusters, share, terms), bf16),
        pltpu.SemaphoreType.DMA((6,)),
    ]
    params = pltpu.CompilerParams(vmem_limit_bytes=VMEM_LIMIT)
    whole = lambda *_: (0, 0, 0, 0)
    near_flops = 2 * clusters * near_count * size * share * terms * groups

    near_send = pl.pallas_call(
        functools.partial(near_kernel, scale, near_cap),
        out_shape=jax.ShapeDtypeStruct((leaf_count, groups, near_cap, share, share), bf16),
        grid_spec=pltpu.PrefetchScalarGridSpec(
            num_scalar_prefetch=4,
            grid=(leaf_count,),
            in_specs=[
                pl.BlockSpec(
                    (groups, clusters, size, terms), whole, pipeline_mode=pl.Buffered(1)
                ),
                *[any_spec] * 6,
            ],
            out_specs=pl.BlockSpec(
                (1, groups, near_cap, share, share), lambda i, *_: (i, 0, 0, 0, 0)
            ),
            scratch_shapes=scratch,
        ),
        compiler_params=params,
        cost_estimate=pl.CostEstimate(
            flops=near_flops, bytes_accessed=18 * 1024 * 1024, transcendentals=0
        ),
        name="near",
    )(near_pick, near_at // near_count, near_column[near_at], order, scaled, *fields)

    far_scaled = after(scaled, near_send)
    all_right = lax.all_gather(after(sketch_right, near_send), "rep", tiled=True)
    got_near = exchange(
        near_send.reshape(leaf_count * groups, near_cap, share, share), ("leaf", "rep")
    ).reshape(leaf_count, groups, near_cap, share, share)

    my_left = lax.dynamic_slice_in_dim(sketch_left, lax.axis_index("rep") * share, share, axis=0)
    left_parts, right_rows = pl.pallas_call(
        functools.partial(far_kernel, scale),
        out_shape=(
            jax.ShapeDtypeStruct((groups, clusters, far_count, share // 2, 2 * width), bf16),
            jax.ShapeDtypeStruct((clusters, far_count, share, width), f32),
        ),
        grid_spec=pltpu.PrefetchScalarGridSpec(
            num_scalar_prefetch=2,
            grid=(clusters,),
            in_specs=[
                pl.BlockSpec(
                    (groups, clusters, size, terms), whole, pipeline_mode=pl.Buffered(1)
                ),
                *[any_spec] * 6,
                pl.BlockSpec((share, width), lambda *_: (0, 0)),
                pl.BlockSpec((size, width), lambda *_: (0, 0)),
            ],
            out_specs=(
                pl.BlockSpec(
                    (groups, 1, far_count, share // 2, 2 * width), lambda i, *_: (0, i, 0, 0, 0)
                ),
                pl.BlockSpec((1, far_count, share, width), lambda i, *_: (i, 0, 0, 0)),
            ),
            scratch_shapes=scratch,
        ),
        compiler_params=params,
        cost_estimate=pl.CostEstimate(
            flops=near_flops, bytes_accessed=16 * 1024 * 1024, transcendentals=0
        ),
        name="far",
    )(far_column, order, far_scaled, *fields, my_left, all_right)

    blocks = clusters * far_count
    left_rows = lax.psum_scatter(left_parts, "rep", scatter_dimension=0, tiled=True)
    far_send = pl.pallas_call(
        functools.partial(join_kernel, far_cap),
        out_shape=jax.ShapeDtypeStruct((leaf_count, far_cap, share, 2 * width), bf16),
        grid_spec=pltpu.PrefetchScalarGridSpec(
            num_scalar_prefetch=2,
            grid=(leaf_count,),
            in_specs=[
                pl.BlockSpec((blocks, share // 2, 2 * width), lambda *_: (0, 0, 0)),
                pl.BlockSpec((blocks, share, width), lambda *_: (0, 0, 0)),
            ],
            out_specs=pl.BlockSpec((1, far_cap, share, 2 * width), lambda i, *_: (i, 0, 0, 0)),
        ),
        compiler_params=params,
        cost_estimate=pl.CostEstimate(
            flops=1 << 20, bytes_accessed=4 * 1024 * 1024, transcendentals=0
        ),
        name="join",
    )(
        far_pick,
        far_rank.reshape(-1)[far_at],
        left_rows.reshape(blocks, share // 2, 2 * width),
        right_rows.reshape(blocks, share, width),
    )
    far_send = after(far_send, got_near)
    got_far = exchange(far_send, "leaf")
    near_out = pl.pallas_call(
        join_columns,
        out_shape=jax.ShapeDtypeStruct((1, leaf_count, near_cap, share, size), bf16),
        grid=(leaf_count,),
        in_specs=[
            pl.BlockSpec((1, groups, near_cap, share, share), lambda i: (i, 0, 0, 0, 0))
        ],
        out_specs=pl.BlockSpec((1, 1, near_cap, share, size), lambda i: (0, i, 0, 0, 0)),
        compiler_params=params,
        cost_estimate=pl.CostEstimate(
            flops=1 << 20, bytes_accessed=12 * 1024 * 1024, transcendentals=0
        ),
        name="columns",
    )(got_near)
    return (near_out, got_far[None])


def solution(mesh):
    in_specs = (
        P("leaf", None, "rep"),
        P("leaf"),
        P("rep"),
        P(),
        P("rep", None),
        P("leaf", None),
        P("leaf", None),
        P("leaf", None),
        P("leaf", None),
        P("leaf", None),
    )
    out_specs = (P("leaf", None, None, "rep", None), P("leaf", None, None, "rep", None))
    return jax.shard_map(local, mesh=mesh, in_specs=in_specs, out_specs=out_specs, check_vma=False)
```

```python
import functools
import math

import jax
import jax.numpy as jnp
from jax import lax
from jax.experimental import pallas as pl
from jax.experimental.pallas import tpu as pltpu
from jax.sharding import PartitionSpec as P

VMEM_LIMIT = 56 * 1024 * 1024


def ranks(owners, leaf_count):
    onehot = (owners[:, None] == jnp.arange(leaf_count, dtype=jnp.int32)[None, :]).astype(jnp.int32)
    return jnp.sum(jnp.cumsum(onehot, axis=0) * onehot, axis=1) - 1


def block_of_slot(owners, capacity, leaf_count):
    slots = owners * capacity + ranks(owners, leaf_count)
    hits = jnp.arange(leaf_count * capacity, dtype=jnp.int32)[:, None] == slots[None, :]
    sources = jnp.arange(owners.shape[0], dtype=jnp.int32)[None, :]
    return jnp.max(jnp.where(hits, sources, -1), axis=1)


def tile(order, scaled_ref, cluster, fields_ref, column, scale):
    total = None
    for group in range(scaled_ref.shape[0]):
        term = lax.dot_general(
            scaled_ref[order[group], cluster],
            fields_ref[column // scaled_ref.shape[1], group, column % scaled_ref.shape[1]],
            (((1,), (1,)), ((), ())),
            preferred_element_type=jnp.float32,
        )
        total = term if total is None else total + term
    summed = total * scale
    return (summed * lax.rsqrt(1.0 + summed * summed)).astype(jnp.bfloat16)


def load_fields(parts, fields, sems):
    copies = []
    for i, part in enumerate(parts):
        if i % 2 == 0:
            target = fields.at[i // 2, 0]
        else:
            target = fields.at[i // 2, pl.ds(1, fields.shape[1] - 1)]
        copies.append(pltpu.make_async_copy(part, target, sems.at[i]))
    for copy in copies:
        copy.start()
    for copy in copies:
        copy.wait()


def near_kernel(scale, cap, pick, cluster, column, order, scaled, *refs):
    parts, (out, fields, sems) = refs[:6], refs[6:]
    step = pl.program_id(0)

    @pl.when(step == 0)
    def _():
        load_fields(parts, fields, sems)

    for slot in range(cap):
        n = step * cap + slot

        @pl.when(pick[n] >= 0)
        def _():
            made = tile(order, scaled, cluster[n], fields, column[n], scale)
            share = out.shape[3]
            for r in range(out.shape[1]):
                out[0, r, slot] = made[r * share : (r + 1) * share]

        @pl.when(pick[n] < 0)
        def _():
            out[0, :, slot] = jnp.zeros((out.shape[1],) + out.shape[3:], out.dtype)


def far_kernel(scale, column, order, scaled, *refs):
    parts, (sk_left, sk_right, left_out, right_out, fields, sems) = refs[:6], refs[6:]
    step = pl.program_id(0)

    @pl.when(step == 0)
    def _():
        load_fields(parts, fields, sems)

    count = right_out.shape[1]
    for f in range(count):
        made = tile(order, scaled, step, fields, column[step * count + f], scale)
        right_out[0, f] = lax.dot_general(
            made, sk_right[...], (((0,), (0,)), ((), ())), preferred_element_type=jnp.float32
        )
        part = jnp.dot(made, sk_left[...], preferred_element_type=jnp.float32).astype(jnp.bfloat16)
        share = made.shape[0] // left_out.shape[0]
        half = share // 2
        for r in range(left_out.shape[0]):
            base = r * share
            left_out[r, 0, f] = jnp.concatenate(
                [part[base : base + half], part[base + half : base + share]], axis=1
            )


def join_kernel(cap, pick, rank, left_rows, right, out):
    step = pl.program_id(0)
    for slot in range(cap):
        n = step * cap + slot

        @pl.when(pick[n] >= 0)
        def _():
            block = pick[n]
            total = left_rows[block].astype(jnp.float32)
            width = total.shape[1] // 2
            left = jnp.concatenate([total[:, :width], total[:, width:]], axis=0)
            both = jnp.concatenate([left, right[block]], axis=1)
            column = lax.broadcasted_iota(jnp.int32, both.shape, 1) % width
            out[0, slot] = jnp.where(column < rank[n], both, 0.0).astype(out.dtype)

        @pl.when(pick[n] < 0)
        def _():
            out[0, slot] = jnp.zeros(out.shape[2:], out.dtype)


def join_columns(got, out):
    share = got.shape[4]
    for r in range(got.shape[1]):
        out[0, 0, :, :, r * share : (r + 1) * share] = got[0, r]


def local(
    panel_feats,
    panel_dest,
    coefs,
    sketch_left,
    sketch_right,
    near_cols,
    far_cols,
    near_owner,
    far_owner,
    far_rank,
):
    bf16, f32 = jnp.bfloat16, jnp.float32
    leaf_count = lax.axis_size("leaf")
    groups = lax.axis_size("rep")
    position = lax.axis_index("leaf")
    panel_rows = panel_feats.shape[0]
    terms = panel_feats.shape[2]
    clusters = near_cols.shape[0]
    near_count = near_cols.shape[1]
    far_count = far_cols.shape[1]
    size = panel_rows // clusters
    share = size // groups
    width = sketch_left.shape[1]
    per_peer = panel_rows // leaf_count
    capacity = per_peer + max(1, per_peer // 4)
    slot_total = leaf_count * capacity
    near_cap = max(2, (2 * clusters * near_count + leaf_count - 1) // leaf_count)
    far_cap = max(2, (2 * clusters * far_count + leaf_count - 1) // leaf_count)
    scale = 1.0 / math.sqrt(terms * groups)

    def exchange(x, axis):
        return lax.all_to_all(x, axis, split_axis=0, concat_axis=0, tiled=True)

    dest_owner = panel_dest // panel_rows
    outgoing = dest_owner * capacity + ranks(dest_owner, leaf_count)
    pack = (jnp.arange(slot_total, dtype=jnp.int32)[:, None] == outgoing[None, :]).astype(bf16)

    def packed(feats):
        rows = jnp.dot(pack, feats, preferred_element_type=f32).astype(bf16)
        return rows.reshape(leaf_count, capacity, terms)

    place = panel_dest % panel_rows
    codes = jnp.stack([place // 128, place % 128, jnp.ones_like(place)], axis=1).astype(bf16)
    sent = jnp.dot(pack, codes, preferred_element_type=f32).astype(jnp.int32)
    send_place = jnp.where(sent[:, 2] > 0, sent[:, 0] * 128 + sent[:, 1], panel_rows)
    got_place = exchange(send_place.reshape(leaf_count, capacity), "leaf").reshape(-1)

    def after(value, earlier):
        return lax.optimization_barrier((value, earlier))[0]

    got_field = exchange(after(packed(panel_feats[:, 1, :]), got_place), "leaf")
    send_source = after(packed(panel_feats[:, 0, :]), got_field)
    got_field = got_field.reshape(slot_total, terms)
    got_source = exchange(send_source, "leaf").reshape(slot_total, terms)
    me = lax.axis_index("rep")
    steps = jnp.arange(groups, dtype=jnp.int32)
    turned = (me + steps) % groups
    order = (me - steps + groups) % groups
    inner = jnp.arange(share, dtype=jnp.int32)
    by_share = (
        jnp.arange(clusters, dtype=jnp.int32)[None, :, None] * size
        + turned[:, None, None] * share
        + inner[None, None, :]
    ).reshape(-1)
    sort_share = (by_share[:, None] == got_place[None, :]).astype(bf16)
    field = jnp.dot(sort_share, got_field, preferred_element_type=f32).astype(bf16)
    field = field.reshape(groups, clusters, share, terms)
    first = field[0]
    rest = jnp.stack(
        [
            lax.ppermute(field[k], "rep", [(i, (i + k) % groups) for i in range(groups)])
            for k in range(1, groups)
        ]
    )
    ends = leaf_count - 1
    up = [(i, i + 1) for i in range(ends)]
    down = [(i + 1, i) for i in range(ends)]
    fields = (
        lax.ppermute(first, "leaf", up),
        lax.ppermute(rest, "leaf", up),
        first,
        rest,
        lax.ppermute(first, "leaf", down),
        lax.ppermute(rest, "leaf", down),
    )
    row = jnp.arange(panel_rows, dtype=jnp.int32)
    sort = (row[:, None] == after(got_place, (rest, fields[0], fields[4]))[None, :]).astype(bf16)
    source = jnp.dot(sort, got_source, preferred_element_type=f32)
    scaled = (source.astype(bf16).astype(f32) * coefs).astype(bf16)
    scaled = lax.all_gather(scaled.reshape(clusters, size, terms), "rep")

    near_column = (near_cols - (position - 1) * clusters).reshape(-1)
    far_column = (far_cols - (position - 1) * clusters).reshape(-1)
    near_pick = block_of_slot(near_owner.reshape(-1), near_cap, leaf_count)
    far_pick = block_of_slot(far_owner.reshape(-1), far_cap, leaf_count)
    near_at = jnp.maximum(near_pick, 0)
    far_at = jnp.maximum(far_pick, 0)
    any_spec = pl.BlockSpec(memory_space=pl.ANY)
    scratch = [
        pltpu.VMEM((3, groups, clusters, share, terms), bf16),
        pltpu.SemaphoreType.DMA((6,)),
    ]
    params = pltpu.CompilerParams(vmem_limit_bytes=VMEM_LIMIT)
    whole = lambda *_: (0, 0, 0, 0)
    near_flops = 2 * clusters * near_count * size * share * terms * groups

    near_send = pl.pallas_call(
        functools.partial(near_kernel, scale, near_cap),
        out_shape=jax.ShapeDtypeStruct((leaf_count, groups, near_cap, share, share), bf16),
        grid_spec=pltpu.PrefetchScalarGridSpec(
            num_scalar_prefetch=4,
            grid=(leaf_count,),
            in_specs=[
                pl.BlockSpec(
                    (groups, clusters, size, terms), whole, pipeline_mode=pl.Buffered(1)
                ),
                *[any_spec] * 6,
            ],
            out_specs=pl.BlockSpec(
                (1, groups, near_cap, share, share), lambda i, *_: (i, 0, 0, 0, 0)
            ),
            scratch_shapes=scratch,
        ),
        compiler_params=params,
        cost_estimate=pl.CostEstimate(
            flops=near_flops, bytes_accessed=18 * 1024 * 1024, transcendentals=0
        ),
        name="near",
    )(near_pick, near_at // near_count, near_column[near_at], order, scaled, *fields)

    far_scaled = after(scaled, near_send)
    all_right = lax.all_gather(after(sketch_right, near_send), "rep", tiled=True)
    got_near = exchange(
        near_send.reshape(leaf_count * groups, near_cap, share, share), ("leaf", "rep")
    ).reshape(leaf_count, groups, near_cap, share, share)

    my_left = lax.dynamic_slice_in_dim(sketch_left, lax.axis_index("rep") * share, share, axis=0)
    left_parts, right_rows = pl.pallas_call(
        functools.partial(far_kernel, scale),
        out_shape=(
            jax.ShapeDtypeStruct((groups, clusters, far_count, share // 2, 2 * width), bf16),
            jax.ShapeDtypeStruct((clusters, far_count, share, width), f32),
        ),
        grid_spec=pltpu.PrefetchScalarGridSpec(
            num_scalar_prefetch=2,
            grid=(clusters,),
            in_specs=[
                pl.BlockSpec(
                    (groups, clusters, size, terms), whole, pipeline_mode=pl.Buffered(1)
                ),
                *[any_spec] * 6,
                pl.BlockSpec((share, width), lambda *_: (0, 0)),
                pl.BlockSpec((size, width), lambda *_: (0, 0)),
            ],
            out_specs=(
                pl.BlockSpec(
                    (groups, 1, far_count, share // 2, 2 * width), lambda i, *_: (0, i, 0, 0, 0)
                ),
                pl.BlockSpec((1, far_count, share, width), lambda i, *_: (i, 0, 0, 0)),
            ),
            scratch_shapes=scratch,
        ),
        compiler_params=params,
        cost_estimate=pl.CostEstimate(
            flops=near_flops, bytes_accessed=16 * 1024 * 1024, transcendentals=0
        ),
        name="far",
    )(far_column, order, far_scaled, *fields, my_left, all_right)

    blocks = clusters * far_count
    left_rows = lax.psum_scatter(left_parts, "rep", scatter_dimension=0, tiled=True)
    far_send = pl.pallas_call(
        functools.partial(join_kernel, far_cap),
        out_shape=jax.ShapeDtypeStruct((leaf_count, far_cap, share, 2 * width), bf16),
        grid_spec=pltpu.PrefetchScalarGridSpec(
            num_scalar_prefetch=2,
            grid=(leaf_count,),
            in_specs=[
                pl.BlockSpec((blocks, share // 2, 2 * width), lambda *_: (0, 0, 0)),
                pl.BlockSpec((blocks, share, width), lambda *_: (0, 0, 0)),
            ],
            out_specs=pl.BlockSpec((1, far_cap, share, 2 * width), lambda i, *_: (i, 0, 0, 0)),
        ),
        compiler_params=params,
        cost_estimate=pl.CostEstimate(
            flops=1 << 20, bytes_accessed=4 * 1024 * 1024, transcendentals=0
        ),
        name="join",
    )(
        far_pick,
        far_rank.reshape(-1)[far_at],
        left_rows.reshape(blocks, share // 2, 2 * width),
        right_rows.reshape(blocks, share, width),
    )
    far_send = after(far_send, got_near)
    got_far = exchange(far_send, "leaf")
    near_out = pl.pallas_call(
        join_columns,
        out_shape=jax.ShapeDtypeStruct((1, leaf_count, near_cap, share, size), bf16),
        grid=(leaf_count,),
        in_specs=[
            pl.BlockSpec((1, groups, near_cap, share, share), lambda i: (i, 0, 0, 0, 0))
        ],
        out_specs=pl.BlockSpec((1, 1, near_cap, share, size), lambda i: (0, i, 0, 0, 0)),
        compiler_params=params,
        cost_estimate=pl.CostEstimate(
            flops=1 << 20, bytes_accessed=12 * 1024 * 1024, transcendentals=0
        ),
        name="columns",
    )(got_near)
    return (near_out, got_far[None])


def solution(mesh):
    in_specs = (
        P("leaf", None, "rep"),
        P("leaf"),
        P("rep"),
        P(),
        P("rep", None),
        P("leaf", None),
        P("leaf", None),
        P("leaf", None),
        P("leaf", None),
        P("leaf", None),
    )
    out_specs = (P("leaf", None, None, "rep", None), P("leaf", None, None, "rep", None))
    return jax.shard_map(local, mesh=mesh, in_specs=in_specs, out_specs=out_specs, check_vma=False)
```

```python
import functools
import math

import jax
import jax.numpy as jnp
from jax import lax
from jax.experimental import pallas as pl
from jax.experimental.pallas import tpu as pltpu
from jax.sharding import PartitionSpec as P

VMEM_LIMIT = 56 * 1024 * 1024


def ranks(owners, leaf_count):
    onehot = (owners[:, None] == jnp.arange(leaf_count, dtype=jnp.int32)[None, :]).astype(jnp.int32)
    return jnp.sum(jnp.cumsum(onehot, axis=0) * onehot, axis=1) - 1


def block_of_slot(owners, capacity, leaf_count):
    slots = owners * capacity + ranks(owners, leaf_count)
    hits = jnp.arange(leaf_count * capacity, dtype=jnp.int32)[:, None] == slots[None, :]
    sources = jnp.arange(owners.shape[0], dtype=jnp.int32)[None, :]
    return jnp.max(jnp.where(hits, sources, -1), axis=1)


def tile(order, scaled_ref, cluster, fields_ref, column, scale):
    total = None
    for group in range(scaled_ref.shape[0]):
        term = lax.dot_general(
            scaled_ref[order[group], cluster],
            fields_ref[column // scaled_ref.shape[1], group, column % scaled_ref.shape[1]],
            (((1,), (1,)), ((), ())),
            preferred_element_type=jnp.float32,
        )
        total = term if total is None else total + term
    summed = total * scale
    return (summed * lax.rsqrt(1.0 + summed * summed)).astype(jnp.bfloat16)


def load_fields(parts, fields, sems):
    copies = []
    for i, part in enumerate(parts):
        if i % 2 == 0:
            target = fields.at[i // 2, 0]
        else:
            target = fields.at[i // 2, pl.ds(1, fields.shape[1] - 1)]
        copies.append(pltpu.make_async_copy(part, target, sems.at[i]))
    for copy in copies:
        copy.start()
    for copy in copies:
        copy.wait()


def near_kernel(scale, cap, base, pick, cluster, column, order, scaled, *refs):
    parts, (out, fields, sems) = refs[:6], refs[6:]
    step = pl.program_id(0)

    @pl.when(step == 0)
    def _():
        load_fields(parts, fields, sems)

    for slot in range(out.shape[2]):
        n = step * cap + base + slot

        @pl.when(pick[n] >= 0)
        def _():
            made = tile(order, scaled, cluster[n], fields, column[n], scale)
            share = out.shape[3]
            for r in range(out.shape[1]):
                out[0, r, slot] = made[r * share : (r + 1) * share]

        @pl.when(pick[n] < 0)
        def _():
            out[0, :, slot] = jnp.zeros((out.shape[1],) + out.shape[3:], out.dtype)


def far_kernel(scale, column, order, scaled, *refs):
    parts, (sk_left, sk_right, left_out, right_out, fields, sems) = refs[:6], refs[6:]
    step = pl.program_id(0)

    @pl.when(step == 0)
    def _():
        load_fields(parts, fields, sems)

    count = right_out.shape[1]
    for f in range(count):
        made = tile(order, scaled, step, fields, column[step * count + f], scale)
        right_out[0, f] = lax.dot_general(
            made, sk_right[...], (((0,), (0,)), ((), ())), preferred_element_type=jnp.float32
        )
        part = jnp.dot(made, sk_left[...], preferred_element_type=jnp.float32).astype(jnp.bfloat16)
        share = made.shape[0] // left_out.shape[0]
        half = share // 2
        for r in range(left_out.shape[0]):
            base = r * share
            left_out[r, 0, f] = jnp.concatenate(
                [part[base : base + half], part[base + half : base + share]], axis=1
            )


def join_kernel(cap, pick, rank, left_rows, right, out):
    step = pl.program_id(0)
    for slot in range(cap):
        n = step * cap + slot

        @pl.when(pick[n] >= 0)
        def _():
            block = pick[n]
            total = left_rows[block].astype(jnp.float32)
            width = total.shape[1] // 2
            left = jnp.concatenate([total[:, :width], total[:, width:]], axis=0)
            both = jnp.concatenate([left, right[block]], axis=1)
            column = lax.broadcasted_iota(jnp.int32, both.shape, 1) % width
            out[0, slot] = jnp.where(column < rank[n], both, 0.0).astype(out.dtype)

        @pl.when(pick[n] < 0)
        def _():
            out[0, slot] = jnp.zeros(out.shape[2:], out.dtype)


def join_columns(low, high, out):
    share, first = low.shape[4], low.shape[2]
    for r in range(low.shape[1]):
        columns = slice(r * share, (r + 1) * share)
        out[0, 0, :first, :, columns] = low[0, r]
        out[0, 0, first:, :, columns] = high[0, r]


def local(
    panel_feats,
    panel_dest,
    coefs,
    sketch_left,
    sketch_right,
    near_cols,
    far_cols,
    near_owner,
    far_owner,
    far_rank,
):
    bf16, f32 = jnp.bfloat16, jnp.float32
    leaf_count = lax.axis_size("leaf")
    groups = lax.axis_size("rep")
    position = lax.axis_index("leaf")
    panel_rows = panel_feats.shape[0]
    terms = panel_feats.shape[2]
    clusters = near_cols.shape[0]
    near_count = near_cols.shape[1]
    far_count = far_cols.shape[1]
    size = panel_rows // clusters
    share = size // groups
    width = sketch_left.shape[1]
    per_peer = panel_rows // leaf_count
    capacity = per_peer + max(1, per_peer // 4)
    slot_total = leaf_count * capacity
    near_cap = max(2, (2 * clusters * near_count + leaf_count - 1) // leaf_count)
    far_cap = max(2, (2 * clusters * far_count + leaf_count - 1) // leaf_count)
    scale = 1.0 / math.sqrt(terms * groups)

    def exchange(x, axis):
        return lax.all_to_all(x, axis, split_axis=0, concat_axis=0, tiled=True)

    dest_owner = panel_dest // panel_rows
    outgoing = dest_owner * capacity + ranks(dest_owner, leaf_count)
    pack = (jnp.arange(slot_total, dtype=jnp.int32)[:, None] == outgoing[None, :]).astype(bf16)

    def packed(feats):
        rows = jnp.dot(pack, feats, preferred_element_type=f32).astype(bf16)
        return rows.reshape(leaf_count, capacity, terms)

    place = panel_dest % panel_rows
    codes = jnp.stack([place // 128, place % 128, jnp.ones_like(place)], axis=1).astype(bf16)
    sent = jnp.dot(pack, codes, preferred_element_type=f32).astype(jnp.int32)
    send_place = jnp.where(sent[:, 2] > 0, sent[:, 0] * 128 + sent[:, 1], panel_rows)
    got_place = exchange(send_place.reshape(leaf_count, capacity), "leaf").reshape(-1)

    def after(value, earlier):
        return lax.optimization_barrier((value, earlier))[0]

    got_field = exchange(after(packed(panel_feats[:, 1, :]), got_place), "leaf")
    send_source = after(packed(panel_feats[:, 0, :]), got_field)
    got_field = got_field.reshape(slot_total, terms)
    got_source = exchange(send_source, "leaf").reshape(slot_total, terms)
    me = lax.axis_index("rep")
    steps = jnp.arange(groups, dtype=jnp.int32)
    turned = (me + steps) % groups
    order = (me - steps + groups) % groups
    inner = jnp.arange(share, dtype=jnp.int32)
    by_share = (
        jnp.arange(clusters, dtype=jnp.int32)[None, :, None] * size
        + turned[:, None, None] * share
        + inner[None, None, :]
    ).reshape(-1)
    sort_share = (by_share[:, None] == got_place[None, :]).astype(bf16)
    field = jnp.dot(sort_share, got_field, preferred_element_type=f32).astype(bf16)
    field = field.reshape(groups, clusters, share, terms)
    first = field[0]
    rest = jnp.stack(
        [
            lax.ppermute(field[k], "rep", [(i, (i + k) % groups) for i in range(groups)])
            for k in range(1, groups)
        ]
    )
    ends = leaf_count - 1
    up = [(i, i + 1) for i in range(ends)]
    down = [(i + 1, i) for i in range(ends)]
    fields = (
        lax.ppermute(first, "leaf", up),
        lax.ppermute(rest, "leaf", up),
        first,
        rest,
        lax.ppermute(first, "leaf", down),
        lax.ppermute(rest, "leaf", down),
    )
    row = jnp.arange(panel_rows, dtype=jnp.int32)
    sort = (row[:, None] == after(got_place, (rest, fields[0], fields[4]))[None, :]).astype(bf16)
    source = jnp.dot(sort, got_source, preferred_element_type=f32)
    scaled = (source.astype(bf16).astype(f32) * coefs).astype(bf16)
    scaled = lax.all_gather(scaled.reshape(clusters, size, terms), "rep")

    near_column = (near_cols - (position - 1) * clusters).reshape(-1)
    far_column = (far_cols - (position - 1) * clusters).reshape(-1)
    near_pick = block_of_slot(near_owner.reshape(-1), near_cap, leaf_count)
    far_pick = block_of_slot(far_owner.reshape(-1), far_cap, leaf_count)
    near_at = jnp.maximum(near_pick, 0)
    far_at = jnp.maximum(far_pick, 0)
    any_spec = pl.BlockSpec(memory_space=pl.ANY)
    scratch = [
        pltpu.VMEM((3, groups, clusters, share, terms), bf16),
        pltpu.SemaphoreType.DMA((6,)),
    ]
    params = pltpu.CompilerParams(vmem_limit_bytes=VMEM_LIMIT)
    whole = lambda *_: (0, 0, 0, 0)
    near_flops = 2 * clusters * near_count * size * share * terms * groups

    def near_part(base, count, scaled):
        made = pl.pallas_call(
        functools.partial(near_kernel, scale, near_cap, base),
        out_shape=jax.ShapeDtypeStruct((leaf_count, groups, count, share, share), bf16),
        grid_spec=pltpu.PrefetchScalarGridSpec(
            num_scalar_prefetch=4,
            grid=(leaf_count,),
            in_specs=[
                pl.BlockSpec(
                    (groups, clusters, size, terms), whole, pipeline_mode=pl.Buffered(1)
                ),
                *[any_spec] * 6,
            ],
            out_specs=pl.BlockSpec(
                (1, groups, count, share, share), lambda i, *_: (i, 0, 0, 0, 0)
            ),
            scratch_shapes=scratch,
        ),
        compiler_params=params,
        cost_estimate=pl.CostEstimate(
            flops=near_flops * count // near_cap, bytes_accessed=18 * 1024 * 1024, transcendentals=0
        ),
        name="near" + str(base),
    )(near_pick, near_at // near_count, near_column[near_at], order, scaled, *fields)
        got = exchange(made.reshape(leaf_count * groups, count, share, share), ("leaf", "rep"))
        return made, got.reshape(leaf_count, groups, count, share, share)

    low = near_cap // 2
    made_low, got_low = near_part(0, low, scaled)
    near_send, got_high = near_part(low, near_cap - low, after(scaled, made_low))
    far_scaled = after(scaled, near_send)
    all_right = lax.all_gather(after(sketch_right, near_send), "rep", tiled=True)

    my_left = lax.dynamic_slice_in_dim(sketch_left, lax.axis_index("rep") * share, share, axis=0)
    left_parts, right_rows = pl.pallas_call(
        functools.partial(far_kernel, scale),
        out_shape=(
            jax.ShapeDtypeStruct((groups, clusters, far_count, share // 2, 2 * width), bf16),
            jax.ShapeDtypeStruct((clusters, far_count, share, width), f32),
        ),
        grid_spec=pltpu.PrefetchScalarGridSpec(
            num_scalar_prefetch=2,
            grid=(clusters,),
            in_specs=[
                pl.BlockSpec(
                    (groups, clusters, size, terms), whole, pipeline_mode=pl.Buffered(1)
                ),
                *[any_spec] * 6,
                pl.BlockSpec((share, width), lambda *_: (0, 0)),
                pl.BlockSpec((size, width), lambda *_: (0, 0)),
            ],
            out_specs=(
                pl.BlockSpec(
                    (groups, 1, far_count, share // 2, 2 * width), lambda i, *_: (0, i, 0, 0, 0)
                ),
                pl.BlockSpec((1, far_count, share, width), lambda i, *_: (i, 0, 0, 0)),
            ),
            scratch_shapes=scratch,
        ),
        compiler_params=params,
        cost_estimate=pl.CostEstimate(
            flops=near_flops, bytes_accessed=16 * 1024 * 1024, transcendentals=0
        ),
        name="far",
    )(far_column, order, far_scaled, *fields, my_left, all_right)

    blocks = clusters * far_count
    left_rows = lax.psum_scatter(left_parts, "rep", scatter_dimension=0, tiled=True)
    far_send = pl.pallas_call(
        functools.partial(join_kernel, far_cap),
        out_shape=jax.ShapeDtypeStruct((leaf_count, far_cap, share, 2 * width), bf16),
        grid_spec=pltpu.PrefetchScalarGridSpec(
            num_scalar_prefetch=2,
            grid=(leaf_count,),
            in_specs=[
                pl.BlockSpec((blocks, share // 2, 2 * width), lambda *_: (0, 0, 0)),
                pl.BlockSpec((blocks, share, width), lambda *_: (0, 0, 0)),
            ],
            out_specs=pl.BlockSpec((1, far_cap, share, 2 * width), lambda i, *_: (i, 0, 0, 0)),
        ),
        compiler_params=params,
        cost_estimate=pl.CostEstimate(
            flops=1 << 20, bytes_accessed=4 * 1024 * 1024, transcendentals=0
        ),
        name="join",
    )(
        far_pick,
        far_rank.reshape(-1)[far_at],
        left_rows.reshape(blocks, share // 2, 2 * width),
        right_rows.reshape(blocks, share, width),
    )
    far_send = after(far_send, got_high)
    got_far = exchange(far_send, "leaf")
    near_out = pl.pallas_call(
        join_columns,
        out_shape=jax.ShapeDtypeStruct((1, leaf_count, near_cap, share, size), bf16),
        grid=(leaf_count,),
        in_specs=[
            pl.BlockSpec((1, groups, low, share, share), lambda i: (i, 0, 0, 0, 0)),
            pl.BlockSpec((1, groups, near_cap - low, share, share), lambda i: (i, 0, 0, 0, 0)),
        ],
        out_specs=pl.BlockSpec((1, 1, near_cap, share, size), lambda i: (0, i, 0, 0, 0)),
        compiler_params=params,
        cost_estimate=pl.CostEstimate(
            flops=1 << 20, bytes_accessed=12 * 1024 * 1024, transcendentals=0
        ),
        name="columns",
    )(got_low, got_high)
    return (near_out, got_far[None])


def solution(mesh):
    in_specs = (
        P("leaf", None, "rep"),
        P("leaf"),
        P("rep"),
        P(),
        P("rep", None),
        P("leaf", None),
        P("leaf", None),
        P("leaf", None),
        P("leaf", None),
        P("leaf", None),
    )
    out_specs = (P("leaf", None, None, "rep", None), P("leaf", None, None, "rep", None))
    return jax.shard_map(local, mesh=mesh, in_specs=in_specs, out_specs=out_specs, check_vma=False)
```
